128 devices in a mesh: grp: 16 (over z, y), tp: 8 (over x, core).
Axes of the slice: x: 4, y: 4, z: 4, core: 2. Of those that a mesh axis runs over, the one named last changes fastest.
Arguments:
- queries: bfloat16 [4096, 8192], P('grp', 'tp'), may hold values from -64 to 64
- row_counts: int32 [16], P('grp'), may hold values from 128 to 256, as said below
- owners: int32 [4096], P('grp'), may hold values from 0 to 15, as said below
- lengths: int32 [4096], P('grp'), may hold values from 1601 to 6404, as said below
- img_keys: bfloat16 [16, 6404, 1024], P('grp', None, 'tp'), may hold values from -12 to 12
- img_values: bfloat16 [16, 6404, 1024], P('grp', None, 'tp'), may hold values from -30 to 30
- out_weight: bfloat16 [8192, 8192], P(None, 'tp'), may hold values from -0.0625 to 0.0625
- gate_scalar: float32 [1], replicated, may hold values from 0.3 to 1.5
Outputs:
- mixed: bfloat16 [4096, 8192], P('grp', 'tp')
The draws below stay inside these ranges and needn't reach their ends.
Inputs may be any that keep to these rules, and one draw needn't show every extreme that they name: `row_counts`: rows of a group with local index below its count are live, the others give zero output; some group is full. `owners`: among the 256 rows of one group at most 32 name the same owner; some owner is named by exactly 32 live rows of every group. `lengths`: a multiple of 1601.
All inputs are finite; a program needn't handle non-finite values.
Results may differ from the reference program's by a relative error of at most 0.0053.
Values may be sent and summed in bfloat16 or wider, within the bound.
No kernel may reach another device: no remote copies, remote signals or barrier semaphores. Data moves between devices by JAX's collectives and lax.ppermute only.
A program may use at most 128 MiB of HBM per device.

```python
import jax
import jax.numpy as jnp
from jax import lax

D = 8192
H = 64
KVH = 8
HD = 128
TILE_TOK = 1601
TILES = 4
IMG_TOK = 6404
ROWS_DEV = 256
CAP = 32
ROWS = 4096
N_GRP = 16


def draw_queries(key, part):
    key = jax.random.fold_in(key, 14)
    first_key = jax.random.fold_in(key, 0)
    values_out = jnp.clip(jax.random.normal(first_key, (ROWS, H * HD)), -6.0, 6.0)
    return values_out.astype(jnp.bfloat16)


def draw_img_keys(key, part):
    key = jax.random.fold_in(key, 15)
    values_out = jnp.clip(2.0 * jax.random.normal(key, (N_GRP, IMG_TOK, KVH * HD)), -12.0, 12.0)
    return values_out.astype(jnp.bfloat16)


def draw_row_counts(key, part):
    key = jax.random.fold_in(key, 11)
    first_key, second_key = jax.random.split(key)
    counted = jax.random.randint(first_key, (N_GRP,), ROWS_DEV // 2, ROWS_DEV + 1)
    full_group = jax.random.randint(second_key, (), 0, N_GRP)
    counted = jnp.where(jnp.arange(N_GRP) == full_group, ROWS_DEV, counted)
    return counted.astype(jnp.int32)


def draw_owners(key, part):
    key = jax.random.fold_in(key, 12)
    keys_all = jax.random.split(key, 5)
    ranking = jax.random.permutation(keys_all[0], N_GRP)
    star_owner = ranking[0]
    candidate_count = max(N_GRP // 4, 1)
    second = ranking[1 + jax.random.randint(keys_all[1], (N_GRP,), 0, candidate_count)]
    token_index = jnp.arange(N_GRP * CAP, dtype=jnp.int32)
    token_owner = token_index // CAP
    noise_score = jax.random.randint(keys_all[2], (N_GRP, N_GRP * CAP), 0, 1 << 17) * 1024 + token_index[None, :]
    favored = (token_owner[None, :] == star_owner) | (token_owner[None, :] == second[:, None])
    scores = noise_score + jnp.where(favored, 1 << 28, 0)
    chosen = lax.top_k(scores, ROWS_DEV)[1] // CAP
    half_rows = ROWS_DEV // 2
    front_part = jax.vmap(jax.random.permutation)(jax.random.split(keys_all[3], N_GRP), chosen[:, :half_rows])
    back_part = jax.vmap(jax.random.permutation)(jax.random.split(keys_all[4], N_GRP), chosen[:, half_rows:])
    return jnp.concatenate([front_part, back_part], axis=1).reshape(-1).astype(jnp.int32)


def draw_lengths(key, part):
    key = jax.random.fold_in(key, 13)
    first_key, second_key = jax.random.split(key)
    tiles_seen = jax.random.randint(first_key, (ROWS,), 1, TILES + 1)
    forced_row = jax.random.randint(second_key, (), 0, ROWS)
    tiles_seen = jnp.where(jnp.arange(ROWS) == forced_row, TILES, tiles_seen)
    return (tiles_seen * TILE_TOK).astype(jnp.int32)


def levels(rng, dims, shards, smallest, high):
    level, own = 1.0, jax.random.fold_in(rng, 6)
    for dim, blocks in shards:
        steps = jnp.exp(jax.random.uniform(jax.random.fold_in(own, dim), (blocks,), jnp.float32, smallest / len(shards), high / len(shards)))
        level = level * jnp.repeat(steps, dims[dim] // blocks).reshape([-1 if axis == dim else 1 for axis in range(len(dims))])
    return level


def noise(own_key, shape, width, most, shards=(), kind=jnp.bfloat16):
    drawn = width * jax.random.normal(own_key, shape, jnp.float32)
    if shards:
        drawn = drawn * levels(own_key, shape, shards, -0.22, 0.18)
    return jnp.clip(drawn, -most, most).astype(kind)


def setup_inputs(seed: int = 0) -> dict:
    streams_of = jax.random.split(jax.random.key(seed), 9)
    return {
        "queries": draw_queries(jax.random.fold_in(streams_of[8], 71), 0),
        "row_counts": draw_row_counts(jax.random.fold_in(streams_of[8], 71), 0),
        "owners": draw_owners(jax.random.fold_in(streams_of[8], 71), 0),
        "lengths": draw_lengths(jax.random.fold_in(streams_of[8], 71), 0),
        "img_keys": draw_img_keys(jax.random.fold_in(streams_of[8], 71), 0),
        "img_values": noise(streams_of[5], (N_GRP, IMG_TOK, KVH * HD), 5.0, 30.0, ((0, 16), (2, 8))),
        "out_weight": noise(streams_of[6], (H * HD, D), (H * HD) ** -0.5, 0.0625, ((1, 8),)),
        "gate_scalar": jnp.clip(jax.random.uniform(streams_of[7], (1,), jnp.float32, 0.3, 1.5), 0.3, 1.5),
    }


def attend(query_block, length_block, key_cache, value_cache):
    share = H // KVH
    count = query_block.shape[0]
    grouped = query_block.reshape(count, KVH, share, HD).astype(jnp.float32)
    scores = jnp.einsum("bkgd,lkd->bkgl", grouped, key_cache) * (HD ** -0.5)
    visible = jnp.arange(IMG_TOK, dtype=jnp.int32)[None, None, None, :] < length_block[:, None, None, None]
    scores = jnp.where(visible, scores, -jnp.inf)
    row_peak = jnp.max(scores, axis=-1, keepdims=True)
    weights = jnp.exp(scores - row_peak)
    total_weight = jnp.sum(weights, axis=-1)
    rounded = lax.optimization_barrier(weights.astype(jnp.bfloat16)).astype(jnp.float32)
    combined = jnp.einsum("bkgl,lkd->bkgd", rounded, value_cache) / total_weight[..., None]
    return combined.astype(jnp.bfloat16).reshape(count, H * HD)


def reference(queries, row_counts, owners, lengths, img_keys, img_values, out_weight, gate_scalar):
    row_total = queries.shape[0]
    slot_total = N_GRP * CAP
    local_index = jnp.arange(row_total, dtype=jnp.int32) % ROWS_DEV
    live_rows = local_index < jnp.repeat(row_counts, ROWS_DEV)

    def per_owner(owner_index):
        chosen = live_rows & (owners == owner_index)
        picked = jnp.nonzero(chosen, size=slot_total, fill_value=0)[0].astype(jnp.int32)
        occupied = jnp.arange(slot_total, dtype=jnp.int32) < jnp.sum(chosen.astype(jnp.int32))
        query_rows = queries[picked].reshape(N_GRP, CAP, H * HD)
        length_rows = jnp.where(occupied, lengths[picked], 1).reshape(N_GRP, CAP)
        key_cache = img_keys[owner_index].reshape(IMG_TOK, KVH, HD).astype(jnp.float32)
        value_cache = img_values[owner_index].reshape(IMG_TOK, KVH, HD).astype(jnp.float32)

        def one_block(block_pair):
            return attend(block_pair[0], block_pair[1], key_cache, value_cache)

        outputs = lax.map(one_block, (query_rows, length_rows)).reshape(slot_total, H * HD)
        return outputs, jnp.where(occupied, picked, row_total).astype(jnp.int32)

    outputs, targets = lax.map(per_owner, jnp.arange(N_GRP, dtype=jnp.int32))
    attention = jnp.zeros((row_total, H * HD), jnp.bfloat16)
    attention = attention.at[targets.reshape(-1)].set(outputs.reshape(-1, H * HD), mode="drop")
    projected = jnp.dot(attention, out_weight, preferred_element_type=jnp.float32)
    return (jnp.tanh(gate_scalar[0]) * projected).astype(jnp.bfloat16)
```

```python
import functools

import jax
import jax.numpy as jnp
from jax import lax
from jax.experimental import pallas as pl
from jax.experimental.pallas import tpu as pltpu
from jax.sharding import PartitionSpec as P

f32, bf16, i32 = jnp.float32, jnp.bfloat16, jnp.int32
HD = 128
CAP = 32
TILE = 1601
TILES = 4
TP = 1664
HUGE = 1e30
VM = pl.BlockSpec(memory_space=pltpu.VMEM)
SM = pl.BlockSpec(memory_space=pltpu.SMEM)


def dispatch_body(owners, lengths, counts, queries, send, back):
    rows = queries.shape[0]
    width = queries.shape[1]
    slots = send.shape[0]
    i = lax.broadcasted_iota(i32, (rows, rows), 0)
    j = lax.broadcasted_iota(i32, (rows, rows), 1)
    own_j = jnp.broadcast_to(owners[...].astype(f32), (rows, rows))
    own_i = own_j.T
    same = (own_i == own_j) & (i < j) & (i < counts[0])
    pos = jnp.sum(jnp.where(same, 1.0, 0.0), axis=0, keepdims=True)
    live = lax.broadcasted_iota(i32, (1, rows), 1) < counts[0]
    target = jnp.where(live, owners[...].astype(f32) * CAP + pos, -1.0)
    slot = lax.broadcasted_iota(i32, (slots, rows), 0).astype(f32)
    pick = jnp.where(jnp.broadcast_to(target, (slots, rows)) == slot, 1.0, 0.0).astype(bf16)
    send[:, :width] = jnp.dot(pick, queries[...], preferred_element_type=f32).astype(bf16)
    seen = sum(jnp.where(lengths[...] > k * TILE, 1.0, 0.0) for k in range(TILES))
    seen = jnp.broadcast_to(seen, (HD, rows)).T.astype(bf16)
    send[:, width:] = jnp.dot(pick, seen, preferred_element_type=f32).astype(bf16)
    target_i = jnp.broadcast_to(target, (HD, rows)).T
    lane = lax.broadcasted_iota(i32, (rows, HD), 1).astype(f32)
    for k in range(slots // HD):
        back[:, k * HD : (k + 1) * HD] = jnp.where(target_i == lane + k * HD, 1.0, 0.0).astype(bf16)


def dispatch(owners, lengths, counts, queries, slots):
    rows, width = queries.shape
    return pl.pallas_call(
        dispatch_body,
        out_shape=(
            jax.ShapeDtypeStruct((slots, width + HD), bf16),
            jax.ShapeDtypeStruct((rows, slots), bf16),
        ),
        in_specs=[VM, VM, SM, VM],
        out_specs=(VM, VM),
        name="dispatch",
    )(owners.reshape(1, rows), lengths.reshape(1, rows), counts, queries)


def attend_body(heads, block, recv, keys, values, out, ordered, result, tiles, acc, top):
    width = heads * HD
    slots = recv.shape[0]
    tile_i = jnp.concatenate([recv[:, width:].astype(f32)] * (slots // HD), axis=1)
    tile_j = tile_i.T
    i = lax.broadcasted_iota(i32, (slots, slots), 0)
    j = lax.broadcasted_iota(i32, (slots, slots), 1)
    before = (tile_i > tile_j) | ((tile_i == tile_j) & (i < j))
    rank = jnp.sum(jnp.where(before, 1.0, 0.0), axis=0, keepdims=True)
    rank = jnp.broadcast_to(rank, (slots, slots))
    sort = jnp.where(rank == i.astype(f32), 1.0, 0.0).astype(bf16)
    ordered[...] = jnp.dot(sort, recv[:, :width], preferred_element_type=f32).astype(bf16)
    tile_sorted = jnp.dot(sort, recv[:, width:], preferred_element_type=f32)
    tiles[...] = tile_sorted
    for b in range(slots // block):
        top[b] = jnp.max(tile_sorted[b * block : b * block + 8, :]).astype(i32)
    result[...] = jnp.zeros_like(result)
    cuts = [(o, min(256, TP - o)) for o in range(0, TP, 256)]

    @pl.loop(0, slots // block)
    def _(b):
        count = top[b]

        @pl.when(count > 0)
        def _():
            first = pl.multiple_of(b * block, block)
            rows = ordered[pl.ds(first, block), :]
            query = jnp.concatenate([rows[:, h * HD : (h + 1) * HD] for h in range(heads)], axis=0)
            scaled = query.astype(f32) * HD ** (-0.5)
            high = scaled.astype(bf16)
            low = (scaled - high.astype(f32)).astype(bf16)
            query = jnp.concatenate([high, low], axis=1)
            seen = jnp.concatenate([tiles[pl.ds(first, block), :]] * heads, axis=0)[:, :1]

            def score(t, o, w):
                return jnp.dot(query, keys[t, :, o : o + w], preferred_element_type=f32)

            shift = jnp.max(score(0, 0, 256), axis=1, keepdims=True)
            acc[...] = jnp.zeros_like(acc)

            @pl.loop(0, count)
            def _(t):
                moved = jnp.where(seen > t.astype(f32), shift, HUGE)
                weights = [jnp.exp(score(t, o, w) - moved).astype(bf16) for o, w in cuts]
                acc[...] += jnp.dot(
                    jnp.concatenate(weights, axis=1), values[t], preferred_element_type=f32
                )

            unsafe = jnp.max(jnp.where(acc[:, HD:] < HUGE, 0.0, 1.0))

            @pl.when(unsafe > 0.0)
            def _():
                acc[...] = jnp.zeros_like(acc)

                def step(t, peak):
                    visible = seen > t.astype(f32)
                    scores = jnp.concatenate([score(t, o, w) for o, w in cuts], axis=1)
                    raised = jnp.maximum(peak, jnp.max(scores, axis=1, keepdims=True))
                    raised = jnp.where(visible, raised, peak)
                    weights = jnp.exp(scores - jnp.where(visible, raised, HUGE)).astype(bf16)
                    acc[...] = acc[...] * jnp.exp(peak - raised) + jnp.dot(
                        weights, values[t], preferred_element_type=f32
                    )
                    return raised

                lax.fori_loop(0, count, step, jnp.full((heads * block, 1), -HUGE, f32))

            total = acc[:, HD:]
            mean = acc[:, :HD] / jnp.where(total > 0.0, total, 1.0)
            mean = jnp.where(total > 0.0, mean, 0.0).astype(bf16)
            for h in range(heads):
                result[pl.ds(first, block), h * HD : (h + 1) * HD] = mean[h * block : (h + 1) * block, :]

    unsort = jnp.where(rank.T == j.astype(f32), 1.0, 0.0).astype(bf16)
    out[...] = jnp.dot(unsort, result[...], preferred_element_type=f32).astype(bf16)


def attend(recv, keys, values, block):
    slots = recv.shape[0]
    width = recv.shape[1] - HD
    heads = width // HD
    return pl.pallas_call(
        functools.partial(attend_body, heads, block),
        out_shape=jax.ShapeDtypeStruct((slots, width), bf16),
        in_specs=[VM] * 3,
        out_specs=VM,
        scratch_shapes=[
            pltpu.VMEM((slots, width), bf16),
            pltpu.VMEM((slots, width), bf16),
            pltpu.VMEM((slots, HD), f32),
            pltpu.VMEM((heads * block, 2 * HD), f32),
            pltpu.SMEM((slots // block,), i32),
        ],
        compiler_params=pltpu.CompilerParams(vmem_limit_bytes=50 * 2**20),
        name="attend",
    )(recv, keys, values)


def restore_body(back, returned, out):
    out[...] = jnp.dot(back[...], returned[...], preferred_element_type=f32).astype(bf16)


def restore(back, returned):
    return pl.pallas_call(
        restore_body,
        out_shape=jax.ShapeDtypeStruct((back.shape[0], returned.shape[1]), bf16),
        in_specs=[VM, VM],
        out_specs=VM,
        name="restore",
    )(back, returned)


def project_body(gate, rows, weight, out, acc):
    k = pl.program_id(0)

    @pl.when(k == 0)
    def _():
        acc[...] = jnp.zeros_like(acc)

    acc[...] += jnp.dot(rows[...], weight[...], preferred_element_type=f32)

    @pl.when(k == pl.num_programs(0) - 1)
    def _():
        out[...] = (gate[0] * acc[...]).astype(bf16)


def project(gate, rows, weight):
    count, depth = rows.shape
    width = weight.shape[1]
    step = 1024
    return pl.pallas_call(
        project_body,
        grid=(depth // step,),
        out_shape=jax.ShapeDtypeStruct((count, width), bf16),
        in_specs=[
            SM,
            pl.BlockSpec((count, step), lambda k: (0, k)),
            pl.BlockSpec((step, width), lambda k: (k, 0)),
        ],
        out_specs=pl.BlockSpec((count, width), lambda k: (0, 0)),
        scratch_shapes=[pltpu.VMEM((count, width), f32)],
        compiler_params=pltpu.CompilerParams(vmem_limit_bytes=32 * 2**20),
        name="project",
    )(gate, rows, weight)


def cache_form(img_keys, img_values):
    keys = img_keys[0].reshape(TILES, TILE, HD)
    values = img_values[0].reshape(TILES, TILE, HD)
    keys = jnp.pad(keys, ((0, 0), (0, TP - TILE), (0, 0)), mode="edge").transpose(0, 2, 1)
    keys = jnp.concatenate([keys, keys], axis=1)
    values = jnp.concatenate([values, jnp.ones_like(values)], axis=2)
    values = jnp.pad(values, ((0, 0), (0, TP - TILE), (0, 0)))
    return keys, values


def shards(queries, row_counts, owners, lengths, img_keys, img_values, out_weight, gate_scalar):
    groups = lax.axis_size("grp")
    slots = groups * CAP
    width = queries.shape[1]
    send, back = dispatch(owners, lengths, row_counts, queries, slots)
    keys, values = cache_form(img_keys, img_values)
    recv = lax.all_to_all(send.reshape(groups, CAP, width + HD), "grp", split_axis=0, concat_axis=0, tiled=True)
    result = attend(recv.reshape(slots, width + HD), keys, values, 64)
    returned = lax.all_to_all(result.reshape(groups, CAP, width), "grp", split_axis=0, concat_axis=0, tiled=True)
    rows = restore(back, returned.reshape(slots, width))
    rows = lax.all_gather(rows, "tp", axis=1, tiled=True)
    return project(jnp.tanh(gate_scalar), rows, out_weight)


def solution(mesh):
    placed = (
        P("grp", "tp"),
        P("grp"),
        P("grp"),
        P("grp"),
        P("grp", None, "tp"),
        P("grp", None, "tp"),
        P(None, "tp"),
        P(),
    )
    return jax.shard_map(
        shards, mesh=mesh, in_specs=placed, out_specs=P("grp", "tp"), check_vma=False
    )
```

```python
import functools

import jax
import jax.numpy as jnp
from jax import lax
from jax.experimental import pallas as pl
from jax.experimental.pallas import tpu as pltpu
from jax.sharding import PartitionSpec as P

f32, bf16, i32 = jnp.float32, jnp.bfloat16, jnp.int32
HD = 128
CAP = 32
TILE = 1601
TILES = 4
TP = 1664
VR = 144
LOG2E = 1.4426950408889634
BLOCK = 128
CUTS = [(o, min(256, TP - o)) for o in range(0, TP, 256)]
HUGE = 1e30
UNROLL = 1
VM = pl.BlockSpec(memory_space=pltpu.VMEM)
SM = pl.BlockSpec(memory_space=pltpu.SMEM)
HB = pl.BlockSpec(memory_space=pltpu.HBM)


def like(shape, kind):
    return jax.ShapeDtypeStruct(shape, kind)


def near(x):
    return pltpu.with_memory_space_constraint(x, pltpu.VMEM)


def far(x):
    return pltpu.with_memory_space_constraint(x, pltpu.HBM)


def dispatch_body(owners, lengths, counts, queries, send, place):
    rows = queries.shape[0]
    slots = send.shape[0]
    width = queries.shape[1]
    i = lax.broadcasted_iota(i32, (rows, rows), 0)
    j = lax.broadcasted_iota(i32, (rows, rows), 1)
    own_j = jnp.broadcast_to(owners[...].astype(f32), (rows, rows))
    same = (own_j.T == own_j) & (i < j) & (i < counts[0])
    pos = jnp.sum(jnp.where(same, 1.0, 0.0), axis=0, keepdims=True)
    live = lax.broadcasted_iota(i32, (1, rows), 1) < counts[0]
    target = jnp.where(live, owners[...].astype(f32) * CAP + pos, -1.0)
    slot = lax.broadcasted_iota(i32, (slots, rows), 0).astype(f32)
    pick = jnp.where(jnp.broadcast_to(target, (slots, rows)) == slot, 1.0, 0.0).astype(bf16)
    send[:, :width] = jnp.dot(pick, queries[...], preferred_element_type=f32).astype(bf16)
    seen = sum(jnp.where(lengths[...] > k * TILE, 1.0, 0.0) for k in range(TILES))
    seen = jnp.broadcast_to(seen, (HD, rows)).T.astype(bf16)
    send[:, width:] = jnp.dot(pick, seen, preferred_element_type=f32).astype(bf16)
    place[...] = jnp.broadcast_to(target, place.shape)


def dispatch(owners, lengths, counts, queries, slots):
    rows, width = queries.shape
    return pl.pallas_call(
        dispatch_body,
        out_shape=[like((slots, width + HD), bf16), pltpu.VMEM((8, rows), f32)],
        in_specs=[VM, VM, SM, VM],
        out_specs=[VM, VM],
        name="dispatch",
    )(owners.reshape(1, rows), lengths.reshape(1, rows), counts, queries)


def cache_body(place, img_keys, img_values, keys, values, back):
    total = img_keys.shape[1]
    row = lax.broadcasted_iota(i32, (TP, HD), 0)
    ones = jnp.where(lax.broadcasted_iota(i32, (VR - HD, TP), 1) < TILE, 1.0, 0.0).astype(bf16)
    for source, is_key in ((img_keys, True), (img_values, False)):
        for t in range(TILES):
            first = t * TILE
            low = first // 16 * 16
            high = min(total, -(-(first + TILE) // 16) * 16)
            x = source[0, low:high, :].astype(f32)
            x = jnp.concatenate([x, jnp.zeros((TP + 16 - (high - low), HD), f32)], axis=0)
            if first != low:
                x = pltpu.roll(x, TP + 16 - (first - low), 0)
            x = x[:TP]
            if is_key:
                x = jnp.where(row < TILE, x, jnp.broadcast_to(x[:1], (TP, HD))) * (LOG2E * HD ** (-0.5))
                high_part = x.astype(bf16)
                keys[t, :, :HD] = high_part
                keys[t, :, HD:] = (x - high_part.astype(f32)).astype(bf16)
            else:
                values[t, :HD, :] = jnp.where(row < TILE, x, 0.0).astype(bf16).T
                values[t, HD:, :] = ones
    rows, slots = back.shape
    target = jnp.broadcast_to(place[:1, :], (HD, rows)).T
    lane = lax.broadcasted_iota(i32, (rows, HD), 1).astype(f32)
    for k in range(slots // HD):
        back[:, k * HD : (k + 1) * HD] = jnp.where(target == lane + k * HD, 1.0, 0.0).astype(bf16)


def cache(place, img_keys, img_values, slots):
    return pl.pallas_call(
        cache_body,
        out_shape=[
            like((TILES, TP, 2 * HD), bf16),
            like((TILES, VR, TP), bf16),
            pltpu.VMEM((place.shape[1], slots), bf16),
        ],
        in_specs=[VM, VM, VM],
        out_specs=[VM] * 3,
        compiler_params=pltpu.CompilerParams(vmem_limit_bytes=32 * 2**20),
        name="cache",
    )(near(place), img_keys, img_values)


def attend_body(heads, recv, keys_far, values_far, out, *scratch):
    keys, values, order, blocked, turned, seen, shift, acc, item_b, item_t, sems = scratch
    fetch_keys = pltpu.make_async_copy(keys_far, keys, sems.at[0])
    fetch_values = pltpu.make_async_copy(values_far, values, sems.at[1])
    fetch_keys.start()
    fetch_values.start()
    slots = recv.shape[0]
    width = heads * HD
    blocks = slots // BLOCK
    lanes = heads * BLOCK
    tile_i = jnp.concatenate([recv[:, width:].astype(f32)] * (slots // HD), axis=1)
    tile_j = tile_i.T
    i = lax.broadcasted_iota(i32, (slots, slots), 0)
    j = lax.broadcasted_iota(i32, (slots, slots), 1)
    before = (tile_j > tile_i) | ((tile_j == tile_i) & (j < i))
    rank = jnp.sum(jnp.where(before, 1.0, 0.0), axis=1, keepdims=True)
    placed = rank == j.astype(f32)
    order[...] = jnp.where(placed, 1.0, 0.0).astype(bf16)
    sorted_tiles = jnp.sum(jnp.where(placed, tile_i, 0.0), axis=0, keepdims=True)
    columns = lax.dot_general(
        recv[:, :width], order[...], (((0,), (0,)), ((), ())), preferred_element_type=f32
    ).astype(bf16)
    count = jnp.int32(0)
    for b in range(blocks):
        mine = sorted_tiles[:, b * BLOCK : (b + 1) * BLOCK]
        for h in range(heads):
            x = columns[h * HD : (h + 1) * HD, b * BLOCK : (b + 1) * BLOCK]
            blocked[b, :HD, h * BLOCK : (h + 1) * BLOCK] = x
            blocked[b, HD:, h * BLOCK : (h + 1) * BLOCK] = x
        seen[b] = jnp.broadcast_to(jnp.concatenate([mine] * heads, axis=1), (8, lanes))
        most = jnp.max(mine).astype(i32)
        for t in range(TILES):
            item_b[count] = b
            item_t[count] = t
            count = count + jnp.where(t < most, 1, 0)
    for u in range(UNROLL):
        item_b[count + u] = 0
        item_t[count + u] = TILES
    acc[...] = jnp.zeros_like(acc)

    def score(t, o, w, query):
        return jnp.dot(keys[t, o : o + w, :], query, preferred_element_type=f32)

    fetch_keys.wait()

    @pl.loop(0, blocks)
    def _(b):
        peak = jnp.max(score(0, 0, 256, blocked[b]), axis=0, keepdims=True)
        shift[b] = jnp.broadcast_to(peak, (8, lanes))

    fetch_values.wait()

    def work(b, t):
        tile = jnp.minimum(t, TILES - 1)
        query = blocked[b]
        moved = jnp.where(seen[b, :1, :] > t.astype(f32), shift[b, :1, :], HUGE)
        weights = [jnp.exp2(score(tile, o, w, query) - moved).astype(bf16) for o, w in CUTS]
        acc[b] += jnp.dot(values[tile], jnp.concatenate(weights, axis=0), preferred_element_type=f32)

    @pl.loop(0, (count + UNROLL - 1) // UNROLL)
    def _(n):
        for u in range(UNROLL):
            work(item_b[UNROLL * n + u], item_t[UNROLL * n + u])

    unsafe = jnp.max(jnp.where(acc[:, HD : HD + 1, :] < HUGE, 0.0, 1.0))

    @pl.when(unsafe > 0.0)
    def _():
        acc[...] = jnp.zeros_like(acc)
        shift[...] = jnp.full(shift.shape, -HUGE, f32)

        @pl.loop(0, count)
        def _(n):
            b, t = item_b[n], item_t[n]
            query = blocked[b]
            visible = seen[b, :1, :] > t.astype(f32)
            peak = shift[b, :1, :]
            scores = jnp.concatenate([score(t, o, w, query) for o, w in CUTS], axis=0)
            raised = jnp.where(visible, jnp.maximum(peak, jnp.max(scores, axis=0, keepdims=True)), peak)
            weights = jnp.exp2(scores - jnp.where(visible, raised, HUGE)).astype(bf16)
            acc[b] = acc[b] * jnp.exp2(peak - raised) + jnp.dot(
                values[t], weights, preferred_element_type=f32
            )
            shift[b] = jnp.broadcast_to(raised, (8, lanes))

    for b in range(blocks):
        total = acc[b, HD : HD + 1, :]
        inverse = jnp.where(total > 0.0, 1.0 / jnp.where(total > 0.0, total, 1.0), 0.0)
        mean = (acc[b, :HD, :] * inverse).astype(bf16)
        for h in range(heads):
            turned[h * HD : (h + 1) * HD, b * BLOCK : (b + 1) * BLOCK] = mean[
                :, h * BLOCK : (h + 1) * BLOCK
            ]
    out[...] = lax.dot_general(
        order[...], turned[...], (((1,), (1,)), ((), ())), preferred_element_type=f32
    ).astype(bf16)


def attend(recv, keys, values):
    slots = recv.shape[0]
    width = recv.shape[1] - HD
    heads = width // HD
    blocks = slots // BLOCK
    lanes = heads * BLOCK
    return pl.pallas_call(
        functools.partial(attend_body, heads),
        out_shape=like((slots, width), bf16),
        in_specs=[VM, HB, HB],
        out_specs=VM,
        scratch_shapes=[
            pltpu.VMEM(keys.shape, bf16),
            pltpu.VMEM(values.shape, bf16),
            pltpu.VMEM((slots, slots), bf16),
            pltpu.VMEM((blocks, 2 * HD, lanes), bf16),
            pltpu.VMEM((width, slots), bf16),
            pltpu.VMEM((blocks, 8, lanes), f32),
            pltpu.VMEM((blocks, 8, lanes), f32),
            pltpu.VMEM((blocks, VR, lanes), f32),
            pltpu.SMEM((blocks * TILES + UNROLL,), i32),
            pltpu.SMEM((blocks * TILES + UNROLL,), i32),
            pltpu.SemaphoreType.DMA((2,)),
        ],
        compiler_params=pltpu.CompilerParams(vmem_limit_bytes=42 * 2**20),
        cost_estimate=pl.CostEstimate(
            flops=4 * slots * heads * TP * TILES * HD,
            bytes_accessed=8 * 2**20,
            transcendentals=slots * heads * TP * TILES,
        ),
        name="attend",
    )(recv, far(keys), far(values))


def restore_body(back, returned, upper, lower):
    rows = jnp.dot(back[...], returned[...], preferred_element_type=f32).astype(bf16)
    half = upper.shape[0]
    upper[...] = rows[:half]
    lower[...] = rows[half:]


def restore(back, returned):
    rows, width = back.shape[0], returned.shape[1]
    return pl.pallas_call(
        restore_body,
        out_shape=[like((rows // 2, width), bf16)] * 2,
        in_specs=[VM, VM],
        out_specs=[VM, VM],
        name="restore",
    )(near(back), returned)


def project_body(count, first, last, starts, gate, weight, *refs):
    pieces = refs[: 2 * count]
    before = None if first else refs[2 * count]
    out, held, rows, sems = refs[-4:]
    half, depth = pieces[0].shape

    def fetch(n):
        start = pl.multiple_of(starts[n], depth)
        return [
            pltpu.make_async_copy(weight.at[pl.ds(start, depth), :], held.at[n], sems.at[3 * n]),
            pltpu.make_async_copy(pieces[2 * n], rows.at[n, pl.ds(0, half), :], sems.at[3 * n + 1]),
            pltpu.make_async_copy(pieces[2 * n + 1], rows.at[n, pl.ds(half, half), :], sems.at[3 * n + 2]),
        ]

    for n in range(count):
        for copy in fetch(n):
            copy.start()
    total = None if first else before[...]
    for n in range(count):
        for copy in fetch(n):
            copy.wait()
        term = jnp.dot(rows[n], held[n], preferred_element_type=f32)
        total = term if total is None else total + term
    out[...] = (gate[0] * total).astype(bf16) if last else total


def project(starts, gate, weight, pieces, before, last):
    count = len(pieces)
    half, depth = pieces[0][0].shape
    width = weight.shape[1]
    given = [jnp.stack(starts).astype(i32), gate, far(weight)]
    given += [far(x) for pair in pieces for x in pair]
    spaces = [SM, SM] + [HB] * (1 + 2 * count)
    if before is not None:
        given.append(near(before))
        spaces.append(VM)
    return pl.pallas_call(
        functools.partial(project_body, count, before is None, last),
        out_shape=like((2 * half, width), bf16) if last else pltpu.VMEM((2 * half, width), f32),
        in_specs=spaces,
        out_specs=VM,
        scratch_shapes=[
            pltpu.VMEM((count, depth, width), bf16),
            pltpu.VMEM((count, 2 * half, depth), bf16),
            pltpu.SemaphoreType.DMA((3 * count,)),
        ],
        compiler_params=pltpu.CompilerParams(vmem_limit_bytes=32 * 2**20),
        name="project",
    )(*given)


def shards(queries, row_counts, owners, lengths, img_keys, img_values, out_weight, gate_scalar):
    groups = lax.axis_size("grp")
    shares = lax.axis_size("tp")
    chips = shares // 2
    slots = groups * CAP
    width = queries.shape[1]
    me = lax.axis_index("tp")
    gate = jnp.tanh(gate_scalar)

    def exchange(x):
        x = x.reshape(groups, CAP, x.shape[1])
        x = lax.all_to_all(x, "grp", split_axis=0, concat_axis=0, tiled=True)
        return x.reshape(slots, x.shape[2])

    def round_chips(x, by):
        return lax.ppermute(x, "tp", [(d, (d + 2 * by) % shares) for d in range(shares)])

    def other_core(x):
        return lax.ppermute(x, "tp", [(d, d ^ 1) for d in range(shares)])

    def start(by, core):
        share = (me - 2 * by) % shares
        return (share ^ core) * width

    def both(pair):
        return [other_core(x) for x in pair]

    send, place = dispatch(owners, lengths, row_counts, queries, slots)
    received = exchange(send)
    keys, values, back = cache(place, img_keys, img_values, slots)
    upper, lower = restore(back, exchange(attend(received, keys, values)))
    back_by = chips - 1
    left_upper, right_lower = round_chips(upper, 1), round_chips(lower, back_by)
    left_lower, right_upper = round_chips(lower, 1), round_chips(upper, back_by)
    across = [round_chips(left_upper, 1), round_chips(right_lower, back_by)]
    own = [upper, lower]
    total = project([start(0, 0), start(0, 1)], gate, out_weight, [own, both(own)], None, False)
    left, right = [left_upper, left_lower], [right_upper, right_lower]
    left, right, total = lax.optimization_barrier((left, right, total))
    total = project(
        [start(1, 0), start(-1, 0), start(1, 1), start(-1, 1)],
        gate,
        out_weight,
        [left, right, both(left), both(right)],
        total,
        False,
    )
    across, total = lax.optimization_barrier((across, total))
    beside = both(across)
    total = project([start(2, 0)], gate, out_weight, [across], total, False)
    return project([start(2, 1)], gate, out_weight, [beside], total, True)


def solution(mesh):
    placed = (
        P("grp", "tp"),
        P("grp"),
        P("grp"),
        P("grp"),
        P("grp", None, "tp"),
        P("grp", None, "tp"),
        P(None, "tp"),
        P(),
    )
    return jax.shard_map(
        shards, mesh=mesh, in_specs=placed, out_specs=P("grp", "tp"), check_vma=False
    )
```

```python
import functools

import jax
import jax.numpy as jnp
from jax import lax
from jax.experimental import pallas as pl
from jax.experimental.pallas import tpu as pltpu
from jax.sharding import PartitionSpec as P

f32, bf16, i32 = jnp.float32, jnp.bfloat16, jnp.int32
HD = 128
CAP = 32
TILE = 1601
TILES = 4
TP = 1664
VR = 144
LOG2E = 1.4426950408889634
BLOCK = 128
CUTS = [(o, min(256, TP - o)) for o in range(0, TP, 256)]
HUGE = 1e30
UNROLL = 2
HALVES = 2
VM = pl.BlockSpec(memory_space=pltpu.VMEM)
SM = pl.BlockSpec(memory_space=pltpu.SMEM)
HB = pl.BlockSpec(memory_space=pltpu.HBM)


def like(shape, kind):
    return jax.ShapeDtypeStruct(shape, kind)


def near(x):
    return pltpu.with_memory_space_constraint(x, pltpu.VMEM)


def far(x):
    return pltpu.with_memory_space_constraint(x, pltpu.HBM)


def dispatch_body(owners, lengths, counts, queries, send, place):
    rows = queries.shape[0]
    slots = send.shape[0]
    width = queries.shape[1]
    i = lax.broadcasted_iota(i32, (rows, rows), 0)
    j = lax.broadcasted_iota(i32, (rows, rows), 1)
    own_j = jnp.broadcast_to(owners[...].astype(f32), (rows, rows))
    same = (own_j.T == own_j) & (i < j) & (i < counts[0])
    pos = jnp.sum(jnp.where(same, 1.0, 0.0), axis=0, keepdims=True)
    live = lax.broadcasted_iota(i32, (1, rows), 1) < counts[0]
    target = jnp.where(live, owners[...].astype(f32) * CAP + pos, -1.0)
    slot = lax.broadcasted_iota(i32, (slots, rows), 0).astype(f32)
    pick = jnp.where(jnp.broadcast_to(target, (slots, rows)) == slot, 1.0, 0.0).astype(bf16)
    send[:, :width] = jnp.dot(pick, queries[...], preferred_element_type=f32).astype(bf16)
    seen = sum(jnp.where(lengths[...] > k * TILE, 1.0, 0.0) for k in range(TILES))
    seen = jnp.broadcast_to(seen, (HD, rows)).T.astype(bf16)
    send[:, width:] = jnp.dot(pick, seen, preferred_element_type=f32).astype(bf16)
    place[...] = jnp.broadcast_to(target, place.shape)


def dispatch(owners, lengths, counts, queries, slots):
    rows, width = queries.shape
    return pl.pallas_call(
        dispatch_body,
        out_shape=[like((slots, width + HD), bf16), pltpu.VMEM((8, rows), f32)],
        in_specs=[VM, VM, SM, VM],
        out_specs=[VM, VM],
        name="dispatch",
    )(owners.reshape(1, rows), lengths.reshape(1, rows), counts, queries)


def cache_body(place, img_keys, img_values, keys, values, back):
    total = img_keys.shape[1]
    row = lax.broadcasted_iota(i32, (TP, HD), 0)
    ones = jnp.where(lax.broadcasted_iota(i32, (VR - HD, TP), 1) < TILE, 1.0, 0.0).astype(bf16)
    for source, is_key in ((img_keys, True), (img_values, False)):
        for t in range(TILES):
            first = t * TILE
            low = first // 16 * 16
            high = min(total, -(-(first + TILE) // 16) * 16)
            x = source[0, low:high, :].astype(f32)
            x = jnp.concatenate([x, jnp.zeros((TP + 16 - (high - low), HD), f32)], axis=0)
            if first != low:
                x = pltpu.roll(x, TP + 16 - (first - low), 0)
            x = x[:TP]
            if is_key:
                x = jnp.where(row < TILE, x, jnp.broadcast_to(x[:1], (TP, HD))) * (LOG2E * HD ** (-0.5))
                high_part = x.astype(bf16)
                keys[t, :, :HD] = high_part
                keys[t, :, HD:] = (x - high_part.astype(f32)).astype(bf16)
            else:
                values[t, :HD, :] = jnp.where(row < TILE, x, 0.0).astype(bf16).T
                values[t, HD:, :] = ones
    rows, slots = back.shape
    target = jnp.broadcast_to(place[:1, :], (HD, rows)).T
    lane = lax.broadcasted_iota(i32, (rows, HD), 1).astype(f32)
    for k in range(slots // HD):
        back[:, k * HD : (k + 1) * HD] = jnp.where(target == lane + k * HD, 1.0, 0.0).astype(bf16)


def cache(place, img_keys, img_values, slots):
    return pl.pallas_call(
        cache_body,
        out_shape=[
            like((TILES, TP, 2 * HD), bf16),
            like((TILES, VR, TP), bf16),
            pltpu.VMEM((place.shape[1], slots), bf16),
        ],
        in_specs=[VM, VM, VM],
        out_specs=[VM] * 3,
        compiler_params=pltpu.CompilerParams(vmem_limit_bytes=32 * 2**20),
        name="cache",
    )(near(place), img_keys, img_values)


def attend_body(heads, half, *refs):
    lead = half == 0
    if lead:
        recv, keys_far, values_far, out, order, tiles_out = refs[:6]
    else:
        recv, order, tiles_in, keys_far, values_far, out = refs[:6]
    keys, values, blocked, turned, seen, shift, acc, item_b, item_t, sems = refs[6:]
    fetch_keys = pltpu.make_async_copy(keys_far, keys, sems.at[0])
    fetch_values = pltpu.make_async_copy(values_far, values, sems.at[1])
    fetch_keys.start()
    fetch_values.start()
    slots = recv.shape[0]
    width = heads * HD
    blocks = slots // BLOCK
    lanes = heads * BLOCK
    if lead:
        tile_i = jnp.concatenate([recv[:, HALVES * width :].astype(f32)] * (slots // HD), axis=1)
        tile_j = tile_i.T
        i = lax.broadcasted_iota(i32, (slots, slots), 0)
        j = lax.broadcasted_iota(i32, (slots, slots), 1)
        before = (tile_j > tile_i) | ((tile_j == tile_i) & (j < i))
        rank = jnp.sum(jnp.where(before, 1.0, 0.0), axis=1, keepdims=True)
        placed = rank == j.astype(f32)
        order[...] = jnp.where(placed, 1.0, 0.0).astype(bf16)
        sorted_tiles = jnp.sum(jnp.where(placed, tile_i, 0.0), axis=0, keepdims=True)
        tiles_out[...] = jnp.broadcast_to(sorted_tiles, tiles_out.shape)
    else:
        sorted_tiles = tiles_in[:1, :]
    columns = lax.dot_general(
        recv[:, half * width : (half + 1) * width], order[...], (((0,), (0,)), ((), ())), preferred_element_type=f32
    ).astype(bf16)
    count = jnp.int32(0)
    for b in range(blocks):
        mine = sorted_tiles[:, b * BLOCK : (b + 1) * BLOCK]
        for h in range(heads):
            x = columns[h * HD : (h + 1) * HD, b * BLOCK : (b + 1) * BLOCK]
            blocked[b, :HD, h * BLOCK : (h + 1) * BLOCK] = x
            blocked[b, HD:, h * BLOCK : (h + 1) * BLOCK] = x
        seen[b] = jnp.broadcast_to(jnp.concatenate([mine] * heads, axis=1), (8, lanes))
        most = jnp.max(mine).astype(i32)
        for t in range(TILES):
            item_b[count] = b
            item_t[count] = t
            count = count + jnp.where(t < most, 1, 0)
    for u in range(UNROLL):
        item_b[count + u] = 0
        item_t[count + u] = TILES
    acc[...] = jnp.zeros_like(acc)

    def score(t, o, w, query):
        return jnp.dot(keys[t, o : o + w, :], query, preferred_element_type=f32)

    fetch_keys.wait()

    @pl.loop(0, blocks)
    def _(b):
        peak = jnp.max(score(0, 0, 256, blocked[b]), axis=0, keepdims=True)
        shift[b] = jnp.broadcast_to(peak, (8, lanes))

    fetch_values.wait()

    def work(b, t):
        tile = jnp.minimum(t, TILES - 1)
        query = blocked[b]
        moved = jnp.where(seen[b, :1, :] > t.astype(f32), shift[b, :1, :], HUGE)
        weights = [jnp.exp2(score(tile, o, w, query) - moved).astype(bf16) for o, w in CUTS]
        acc[b] += jnp.dot(values[tile], jnp.concatenate(weights, axis=0), preferred_element_type=f32)

    @pl.loop(0, (count + UNROLL - 1) // UNROLL)
    def _(n):
        for u in range(UNROLL):
            work(item_b[UNROLL * n + u], item_t[UNROLL * n + u])

    unsafe = jnp.max(jnp.where(acc[:, HD : HD + 1, :] < HUGE, 0.0, 1.0))

    @pl.when(unsafe > 0.0)
    def _():
        acc[...] = jnp.zeros_like(acc)
        shift[...] = jnp.full(shift.shape, -HUGE, f32)

        @pl.loop(0, count)
        def _(n):
            b, t = item_b[n], item_t[n]
            query = blocked[b]
            visible = seen[b, :1, :] > t.astype(f32)
            peak = shift[b, :1, :]
            scores = jnp.concatenate([score(t, o, w, query) for o, w in CUTS], axis=0)
            raised = jnp.where(visible, jnp.maximum(peak, jnp.max(scores, axis=0, keepdims=True)), peak)
            weights = jnp.exp2(scores - jnp.where(visible, raised, HUGE)).astype(bf16)
            acc[b] = acc[b] * jnp.exp2(peak - raised) + jnp.dot(
                values[t], weights, preferred_element_type=f32
            )
            shift[b] = jnp.broadcast_to(raised, (8, lanes))

    for b in range(blocks):
        total = acc[b, HD : HD + 1, :]
        inverse = jnp.where(total > 0.0, 1.0 / jnp.where(total > 0.0, total, 1.0), 0.0)
        mean = (acc[b, :HD, :] * inverse).astype(bf16)
        for h in range(heads):
            turned[h * HD : (h + 1) * HD, b * BLOCK : (b + 1) * BLOCK] = mean[
                :, h * BLOCK : (h + 1) * BLOCK
            ]
    out[...] = lax.dot_general(
        order[...], turned[...], (((1,), (1,)), ((), ())), preferred_element_type=f32
    ).astype(bf16)


def attend(half, recv, sorting, keys, values):
    slots = recv.shape[0]
    width = (recv.shape[1] - HD) // HALVES
    heads = width // HD
    blocks = slots // BLOCK
    lanes = heads * BLOCK
    outs = [like((slots, width), bf16)]
    if half == 0:
        outs += [like((slots, slots), bf16), like((8, slots), f32)]
    return pl.pallas_call(
        functools.partial(attend_body, heads, half),
        out_shape=outs,
        in_specs=[VM] * (1 + len(sorting)) + [HB, HB],
        out_specs=[VM] * len(outs),
        scratch_shapes=[
            pltpu.VMEM(keys.shape, bf16),
            pltpu.VMEM(values.shape, bf16),
            pltpu.VMEM((blocks, 2 * HD, lanes), bf16),
            pltpu.VMEM((width, slots), bf16),
            pltpu.VMEM((blocks, 8, lanes), f32),
            pltpu.VMEM((blocks, 8, lanes), f32),
            pltpu.VMEM((blocks, VR, lanes), f32),
            pltpu.SMEM((blocks * TILES + UNROLL,), i32),
            pltpu.SMEM((blocks * TILES + UNROLL,), i32),
            pltpu.SemaphoreType.DMA((2,)),
        ],
        compiler_params=pltpu.CompilerParams(vmem_limit_bytes=42 * 2**20),
        cost_estimate=pl.CostEstimate(
            flops=4 * slots * heads * TP * TILES * HD,
            bytes_accessed=8 * 2**20,
            transcendentals=slots * heads * TP * TILES,
        ),
        name="attend",
    )(recv, *sorting, far(keys), far(values))


def restore_body(back, returned, out):
    out[...] = jnp.dot(back[...], returned[...], preferred_element_type=f32).astype(bf16)


def restore(back, returned):
    return pl.pallas_call(
        restore_body,
        out_shape=pltpu.VMEM((back.shape[0], returned.shape[1]), bf16),
        in_specs=[VM, VM],
        out_specs=VM,
        cost_estimate=pl.CostEstimate(flops=1, bytes_accessed=1, transcendentals=0),
        name="restore",
    )(near(back), near(returned))


def project_body(count, first, last, starts, gate, weight, *refs):
    pieces = refs[:count]
    before = None if first else refs[count]
    out, held, sems = refs[-3:]
    depth = pieces[0].shape[1]

    def fetch(n):
        start = pl.multiple_of(starts[n], depth)
        return pltpu.make_async_copy(weight.at[pl.ds(start, depth), :], held.at[n], sems.at[n])

    for n in range(count):
        fetch(n).start()
    total = None if first else before[...]
    for n in range(count):
        fetch(n).wait()
        term = jnp.dot(pieces[n][...], held[n], preferred_element_type=f32)
        total = term if total is None else total + term
    out[...] = (gate[0] * total).astype(bf16) if last else total


def project(starts, gate, weight, pieces, before, last):
    count = len(pieces)
    rows, depth = pieces[0].shape
    width = weight.shape[1]
    given = [jnp.stack(starts).astype(i32), gate, far(weight), *[near(x) for x in pieces]]
    if before is not None:
        given.append(near(before))
    return pl.pallas_call(
        functools.partial(project_body, count, before is None, last),
        out_shape=like((rows, width), bf16) if last else pltpu.VMEM((rows, width), f32),
        in_specs=[SM, SM, HB] + [VM] * (len(given) - 3),
        out_specs=VM,
        scratch_shapes=[
            pltpu.VMEM((count, depth, width), bf16),
            pltpu.SemaphoreType.DMA((count,)),
        ],
        compiler_params=pltpu.CompilerParams(vmem_limit_bytes=24 * 2**20),
        cost_estimate=pl.CostEstimate(flops=1, bytes_accessed=1, transcendentals=0),
        name="project",
    )(*given)


def shards(queries, row_counts, owners, lengths, img_keys, img_values, out_weight, gate_scalar):
    groups = lax.axis_size("grp")
    shares = lax.axis_size("tp")
    chips = shares // 2
    slots = groups * CAP
    width = queries.shape[1]
    me = lax.axis_index("tp")
    gate = jnp.tanh(gate_scalar)

    def exchange(x):
        x = x.reshape(groups, CAP, x.shape[1])
        x = lax.all_to_all(x, "grp", split_axis=0, concat_axis=0, tiled=True)
        return x.reshape(slots, x.shape[2])

    def round_chips(x, by):
        return lax.ppermute(x, "tp", [(d, (d + 2 * by) % shares) for d in range(shares)])

    def other_core(x):
        return lax.ppermute(x, "tp", [(d, d ^ 1) for d in range(shares)])

    part = width // HALVES

    def start(by, core, half):
        share = (me - 2 * by) % shares
        return (share ^ core) * width + half * part

    def spread(rows):
        return [round_chips(rows, by) for by in hops]

    def add(bys, cores, half, pieces, total, last=False):
        starts = [start(by, core, half) for by, core in zip(bys, cores)]
        return project(starts, gate, out_weight, pieces, total, last)

    hops = (2, 1, chips - 1)
    send, place = dispatch(owners, lengths, row_counts, queries, slots)
    received = exchange(send)
    keys, values, back = cache(place, img_keys, img_values, slots)
    result, *sorting = attend(0, received, [], keys, values)
    first = exchange(result)
    (result,) = attend(1, received, sorting, keys, values)
    first, result = lax.optimization_barrier((first, result))
    second = exchange(result)
    rows = restore(back, first)
    pieces = [rows] + spread(rows)
    rows = restore(back, second)
    again = spread(rows)
    pieces, _ = lax.optimization_barrier((pieces, rows))
    total = add((0,) + hops, (0,) * 4, 0, pieces, None)
    pieces = [other_core(x) for x in pieces]
    total = add((0,) + hops, (1,) * 4, 0, pieces, total)
    total = add((0, 0), (0, 1), 1, [rows, other_core(rows)], total)
    again, total = lax.optimization_barrier((again, total))
    again += [other_core(x) for x in again]
    return add(hops + hops, (0,) * 3 + (1,) * 3, 1, again, total, True)


def solution(mesh):
    placed = (
        P("grp", "tp"),
        P("grp"),
        P("grp"),
        P("grp"),
        P("grp", None, "tp"),
        P("grp", None, "tp"),
        P(None, "tp"),
        P(),
    )
    return jax.shard_map(
        shards, mesh=mesh, in_specs=placed, out_specs=P("grp", "tp"), check_vma=False
    )
```

```python
import functools

import jax
import jax.numpy as jnp
from jax import lax
from jax.experimental import pallas as pl
from jax.experimental.pallas import tpu as pltpu
from jax.sharding import PartitionSpec as P

f32, bf16, i32 = jnp.float32, jnp.bfloat16, jnp.int32
HD = 128
CAP = 32
TILE = 1601
TILES = 4
TP = 1664
VR = 144
LOG2E = 1.4426950408889634
BLOCK = 128
CUTS = [(o, min(256, TP - o)) for o in range(0, TP, 256)]
HUGE = 1e30
HALVES = 2
VM = pl.BlockSpec(memory_space=pltpu.VMEM)
SM = pl.BlockSpec(memory_space=pltpu.SMEM)
HB = pl.BlockSpec(memory_space=pltpu.HBM)


def like(shape, kind):
    return jax.ShapeDtypeStruct(shape, kind)


def near(x):
    return pltpu.with_memory_space_constraint(x, pltpu.VMEM)


def far(x):
    return pltpu.with_memory_space_constraint(x, pltpu.HBM)


def dispatch_body(owners, lengths, counts, queries, send, place):
    rows = queries.shape[0]
    slots = send.shape[0]
    width = queries.shape[1]
    i = lax.broadcasted_iota(i32, (rows, rows), 0)
    j = lax.broadcasted_iota(i32, (rows, rows), 1)
    own_j = jnp.broadcast_to(owners[...].astype(f32), (rows, rows))
    same = (own_j.T == own_j) & (i < j) & (i < counts[0])
    pos = jnp.sum(jnp.where(same, 1.0, 0.0), axis=0, keepdims=True)
    live = lax.broadcasted_iota(i32, (1, rows), 1) < counts[0]
    target = jnp.where(live, owners[...].astype(f32) * CAP + pos, -1.0)
    slot = lax.broadcasted_iota(i32, (slots, rows), 0).astype(f32)
    pick = jnp.where(jnp.broadcast_to(target, (slots, rows)) == slot, 1.0, 0.0).astype(bf16)
    send[:, :width] = jnp.dot(pick, queries[...], preferred_element_type=f32).astype(bf16)
    seen = sum(jnp.where(lengths[...] > k * TILE, 1.0, 0.0) for k in range(TILES))
    seen = jnp.broadcast_to(seen, (HD, rows)).T.astype(bf16)
    send[:, width:] = jnp.dot(pick, seen, preferred_element_type=f32).astype(bf16)
    place[...] = jnp.broadcast_to(target, place.shape)


def dispatch(owners, lengths, counts, queries, slots):
    rows, width = queries.shape
    return pl.pallas_call(
        dispatch_body,
        out_shape=[like((slots, width + HD), bf16), pltpu.VMEM((8, rows), f32)],
        in_specs=[VM, VM, SM, VM],
        out_specs=[VM, VM],
        name="dispatch",
    )(owners.reshape(1, rows), lengths.reshape(1, rows), counts, queries)


def cache_body(place, img_keys, img_values, keys, values, back):
    total = img_keys.shape[1]
    row = lax.broadcasted_iota(i32, (TP, HD), 0)
    ones = jnp.where(lax.broadcasted_iota(i32, (VR - HD, TP), 1) < TILE, 1.0, 0.0).astype(bf16)
    for source, is_key in ((img_keys, True), (img_values, False)):
        for t in range(TILES):
            first = t * TILE
            low = first // 16 * 16
            high = min(total, -(-(first + TILE) // 16) * 16)
            x = source[0, low:high, :].astype(f32)
            x = jnp.concatenate([x, jnp.zeros((TP + 16 - (high - low), HD), f32)], axis=0)
            if first != low:
                x = pltpu.roll(x, TP + 16 - (first - low), 0)
            x = x[:TP]
            if is_key:
                x = jnp.where(row < TILE, x, jnp.broadcast_to(x[:1], (TP, HD))) * (LOG2E * HD ** (-0.5))
                high_part = x.astype(bf16)
                keys[t, :, :HD] = high_part
                keys[t, :, HD:] = (x - high_part.astype(f32)).astype(bf16)
            else:
                values[t, :HD, :] = jnp.where(row < TILE, x, 0.0).astype(bf16).T
                values[t, HD:, :] = ones
    rows, slots = back.shape
    target = jnp.broadcast_to(place[:1, :], (HD, rows)).T
    lane = lax.broadcasted_iota(i32, (rows, HD), 1).astype(f32)
    for k in range(slots // HD):
        back[:, k * HD : (k + 1) * HD] = jnp.where(target == lane + k * HD, 1.0, 0.0).astype(bf16)


def cache(place, img_keys, img_values, slots):
    return pl.pallas_call(
        cache_body,
        out_shape=[
            like((TILES, TP, 2 * HD), bf16),
            like((TILES, VR, TP), bf16),
            pltpu.VMEM((place.shape[1], slots), bf16),
        ],
        in_specs=[VM, VM, VM],
        out_specs=[VM] * 3,
        compiler_params=pltpu.CompilerParams(vmem_limit_bytes=32 * 2**20),
        name="cache",
    )(near(place), img_keys, img_values)


def attend_body(heads, half, *refs):
    lead = half == 0
    if lead:
        recv, keys_far, values_far, out, order, tiles_out = refs[:6]
    else:
        recv, order, tiles_in, keys_far, values_far, out = refs[:6]
    keys, values, blocked, turned, seen, shift, acc, item_b, item_t, sems = refs[6:]
    fetch_keys = pltpu.make_async_copy(keys_far, keys, sems.at[0])
    fetch_values = pltpu.make_async_copy(values_far, values, sems.at[1])
    fetch_keys.start()
    fetch_values.start()
    slots = recv.shape[0]
    width = heads * HD
    blocks = slots // BLOCK
    lanes = heads * BLOCK
    if lead:
        tile_i = jnp.concatenate([recv[:, HALVES * width :].astype(f32)] * (slots // HD), axis=1)
        tile_j = tile_i.T
        i = lax.broadcasted_iota(i32, (slots, slots), 0)
        j = lax.broadcasted_iota(i32, (slots, slots), 1)
        before = (tile_j > tile_i) | ((tile_j == tile_i) & (j < i))
        rank = jnp.sum(jnp.where(before, 1.0, 0.0), axis=1, keepdims=True)
        placed = rank == j.astype(f32)
        order[...] = jnp.where(placed, 1.0, 0.0).astype(bf16)
        sorted_tiles = jnp.sum(jnp.where(placed, tile_i, 0.0), axis=0, keepdims=True)
        tiles_out[...] = jnp.broadcast_to(sorted_tiles, tiles_out.shape)
    else:
        sorted_tiles = tiles_in[:1, :]
    columns = lax.dot_general(
        recv[:, half * width : (half + 1) * width], order[...], (((0,), (0,)), ((), ())), preferred_element_type=f32
    ).astype(bf16)
    count = jnp.int32(0)
    for b in range(blocks):
        mine = sorted_tiles[:, b * BLOCK : (b + 1) * BLOCK]
        for h in range(heads):
            x = columns[h * HD : (h + 1) * HD, b * BLOCK : (b + 1) * BLOCK]
            blocked[b, :HD, h * BLOCK : (h + 1) * BLOCK] = x
            blocked[b, HD:, h * BLOCK : (h + 1) * BLOCK] = x
        seen[b] = jnp.broadcast_to(jnp.concatenate([mine] * heads, axis=1), (8, lanes))
        most = jnp.max(mine).astype(i32)
        for t in range(TILES):
            item_b[count] = b
            item_t[count] = t
            count = count + jnp.where(t < most, 1, 0)
    acc[...] = jnp.zeros_like(acc)

    def score(t, o, w, query):
        return jnp.dot(keys[t, o : o + w, :], query, preferred_element_type=f32)

    fetch_keys.wait()

    @pl.loop(0, blocks)
    def _(b):
        peak = jnp.max(score(0, 0, 256, blocked[b]), axis=0, keepdims=True)
        shift[b] = jnp.broadcast_to(peak, (8, lanes))

    fetch_values.wait()

    def work(b, t):
        query = blocked[b]
        moved = jnp.where(seen[b, :1, :] > t.astype(f32), shift[b, :1, :], HUGE)
        weights = [jnp.exp2(score(t, o, w, query) - moved).astype(bf16) for o, w in CUTS]
        acc[b] += jnp.dot(values[t], jnp.concatenate(weights, axis=0), preferred_element_type=f32)

    @pl.loop(0, count // 2)
    def _(n):
        for u in range(2):
            work(item_b[2 * n + u], item_t[2 * n + u])

    @pl.when(count % 2 == 1)
    def _():
        work(item_b[count - 1], item_t[count - 1])


    unsafe = jnp.max(jnp.where(acc[:, HD : HD + 1, :] < HUGE, 0.0, 1.0))

    @pl.when(unsafe > 0.0)
    def _():
        acc[...] = jnp.zeros_like(acc)
        shift[...] = jnp.full(shift.shape, -HUGE, f32)

        @pl.loop(0, count)
        def _(n):
            b, t = item_b[n], item_t[n]
            query = blocked[b]
            visible = seen[b, :1, :] > t.astype(f32)
            peak = shift[b, :1, :]
            scores = jnp.concatenate([score(t, o, w, query) for o, w in CUTS], axis=0)
            raised = jnp.where(visible, jnp.maximum(peak, jnp.max(scores, axis=0, keepdims=True)), peak)
            weights = jnp.exp2(scores - jnp.where(visible, raised, HUGE)).astype(bf16)
            acc[b] = acc[b] * jnp.exp2(peak - raised) + jnp.dot(
                values[t], weights, preferred_element_type=f32
            )
            shift[b] = jnp.broadcast_to(raised, (8, lanes))

    for b in range(blocks):
        total = acc[b, HD : HD + 1, :]
        inverse = jnp.where(total > 0.0, 1.0 / jnp.where(total > 0.0, total, 1.0), 0.0)
        mean = (acc[b, :HD, :] * inverse).astype(bf16)
        for h in range(heads):
            turned[h * HD : (h + 1) * HD, b * BLOCK : (b + 1) * BLOCK] = mean[
                :, h * BLOCK : (h + 1) * BLOCK
            ]
    out[...] = lax.dot_general(
        order[...], turned[...], (((1,), (1,)), ((), ())), preferred_element_type=f32
    ).astype(bf16)


def attend(half, recv, sorting, keys, values):
    slots = recv.shape[0]
    width = (recv.shape[1] - HD) // HALVES
    heads = width // HD
    blocks = slots // BLOCK
    lanes = heads * BLOCK
    outs = [like((slots, width), bf16)]
    if half == 0:
        outs += [like((slots, slots), bf16), like((8, slots), f32)]
    return pl.pallas_call(
        functools.partial(attend_body, heads, half),
        out_shape=outs,
        in_specs=[VM] * (1 + len(sorting)) + [HB, HB],
        out_specs=[VM] * len(outs),
        scratch_shapes=[
            pltpu.VMEM(keys.shape, bf16),
            pltpu.VMEM(values.shape, bf16),
            pltpu.VMEM((blocks, 2 * HD, lanes), bf16),
            pltpu.VMEM((width, slots), bf16),
            pltpu.VMEM((blocks, 8, lanes), f32),
            pltpu.VMEM((blocks, 8, lanes), f32),
            pltpu.VMEM((blocks, VR, lanes), f32),
            pltpu.SMEM((blocks * TILES + 1,), i32),
            pltpu.SMEM((blocks * TILES + 1,), i32),
            pltpu.SemaphoreType.DMA((2,)),
        ],
        compiler_params=pltpu.CompilerParams(vmem_limit_bytes=42 * 2**20),
        cost_estimate=pl.CostEstimate(
            flops=4 * slots * heads * TP * TILES * HD,
            bytes_accessed=8 * 2**20,
            transcendentals=slots * heads * TP * TILES,
        ),
        name="attend",
    )(recv, *sorting, far(keys), far(values))


def restore_body(back, returned, out):
    out[...] = jnp.dot(back[...], returned[...], preferred_element_type=f32).astype(bf16)


def restore(back, returned):
    return pl.pallas_call(
        restore_body,
        out_shape=pltpu.VMEM((back.shape[0], returned.shape[1]), bf16),
        in_specs=[VM, VM],
        out_specs=VM,
        cost_estimate=pl.CostEstimate(flops=1, bytes_accessed=1, transcendentals=0),
        name="restore",
    )(near(back), near(returned))


def project_body(count, first, last, starts, gate, weight, *refs):
    pieces = refs[:count]
    before = None if first else refs[count]
    out, held, sems = refs[-3:]
    depth = pieces[0].shape[1]

    def fetch(n):
        start = pl.multiple_of(starts[n], depth)
        return pltpu.make_async_copy(weight.at[pl.ds(start, depth), :], held.at[n], sems.at[n])

    for n in range(count):
        fetch(n).start()
    total = None if first else before[...]
    for n in range(count):
        fetch(n).wait()
        term = jnp.dot(pieces[n][...], held[n], preferred_element_type=f32)
        total = term if total is None else total + term
    out[...] = (gate[0] * total).astype(bf16) if last else total


def project(starts, gate, weight, pieces, before, last):
    count = len(pieces)
    rows, depth = pieces[0].shape
    width = weight.shape[1]
    given = [jnp.stack(starts).astype(i32), gate, far(weight), *[near(x) for x in pieces]]
    if before is not None:
        given.append(near(before))
    return pl.pallas_call(
        functools.partial(project_body, count, before is None, last),
        out_shape=like((rows, width), bf16) if last else pltpu.VMEM((rows, width), f32),
        in_specs=[SM, SM, HB] + [VM] * (len(given) - 3),
        out_specs=VM,
        scratch_shapes=[
            pltpu.VMEM((count, depth, width), bf16),
            pltpu.SemaphoreType.DMA((count,)),
        ],
        compiler_params=pltpu.CompilerParams(vmem_limit_bytes=24 * 2**20),
        cost_estimate=pl.CostEstimate(flops=1, bytes_accessed=1, transcendentals=0),
        name="project",
    )(*given)


def shards(queries, row_counts, owners, lengths, img_keys, img_values, out_weight, gate_scalar):
    groups = lax.axis_size("grp")
    shares = lax.axis_size("tp")
    chips = shares // 2
    slots = groups * CAP
    width = queries.shape[1]
    me = lax.axis_index("tp")
    gate = jnp.tanh(gate_scalar)

    def exchange(x):
        x = x.reshape(groups, CAP, x.shape[1])
        x = lax.all_to_all(x, "grp", split_axis=0, concat_axis=0, tiled=True)
        return x.reshape(slots, x.shape[2])

    def round_chips(x, by):
        return lax.ppermute(x, "tp", [(d, (d + 2 * by) % shares) for d in range(shares)])

    def other_core(x):
        return lax.ppermute(x, "tp", [(d, d ^ 1) for d in range(shares)])

    part = width // HALVES

    def start(by, core, half):
        share = (me - 2 * by) % shares
        return (share ^ core) * width + half * part

    def spread(rows):
        return [round_chips(rows, by) for by in hops]

    def add(bys, cores, half, pieces, total, last=False):
        starts = [start(by, core, half) for by, core in zip(bys, cores)]
        return project(starts, gate, out_weight, pieces, total, last)

    hops = (2, 1, chips - 1)
    send, place = dispatch(owners, lengths, row_counts, queries, slots)
    received = exchange(send)
    keys, values, back = cache(place, img_keys, img_values, slots)
    result, *sorting = attend(0, received, [], keys, values)
    first = exchange(result)
    (result,) = attend(1, received, sorting, keys, values)
    first, result = lax.optimization_barrier((first, result))
    second = exchange(result)
    rows = restore(back, first)
    pieces = [rows] + spread(rows)
    rows = restore(back, second)
    again = spread(rows)
    pieces, _ = lax.optimization_barrier((pieces, rows))
    total = add((0,) + hops, (0,) * 4, 0, pieces, None)
    pieces = [other_core(x) for x in pieces]
    total = add((0,) + hops, (1,) * 4, 0, pieces, total)
    total = add((0, 0), (0, 1), 1, [rows, other_core(rows)], total)
    again, total = lax.optimization_barrier((again, total))
    again += [other_core(x) for x in again]
    return add(hops + hops, (0,) * 3 + (1,) * 3, 1, again, total, True)


def solution(mesh):
    placed = (
        P("grp", "tp"),
        P("grp"),
        P("grp"),
        P("grp"),
        P("grp", None, "tp"),
        P("grp", None, "tp"),
        P(None, "tp"),
        P(),
    )
    return jax.shard_map(
        shards, mesh=mesh, in_specs=placed, out_specs=P("grp", "tp"), check_vma=False
    )
```
